256 devices in a mesh: pipe: 32 (over z, x_hi, core), tensor: 8 (over x_lo, y).
Axes of the slice: x: 4 (x_hi: 2, x_lo: 2; x = x_hi * 2 + x_lo), y: 4, z: 8, core: 2. Of those that a mesh axis runs over, the one named last changes fastest.
Arguments:
- hidden: bfloat16 [12288, 14784], P('pipe', 'tensor'), may hold values from -6 to 6
- down_weight: bfloat16 [14784, 4096], P('tensor', 'pipe'), may hold values from -0.046875 to 0.046875
- adapter_in: bfloat16 [16, 14784], P(None, 'tensor'), may hold values from -0.046875 to 0.046875
- adapter_out: bfloat16 [16, 4096], P(None, 'pipe'), may hold values from -0.09375 to 0.09375
- cotangent: bfloat16 [12288, 4096], P('pipe', 'tensor'), may hold values from -6 to 6
Outputs:
- projected: bfloat16 [12288, 4096], P('pipe', 'tensor')
- hidden_gradient: bfloat16 [12288, 14784], P('pipe', 'tensor')
- grad_in: float32 [16, 14784], P(None, 'tensor')
- grad_out: float32 [16, 4096], P(None, 'tensor')
The draws below stay inside these ranges and needn't reach their ends.
All inputs are finite; a program needn't handle non-finite values.
Results may differ from the reference program's by a relative error of at most 0.0034.
Values may be sent and summed in bfloat16 or wider, within the bound.
No kernel may reach another device: no remote copies, remote signals or barrier semaphores. Data moves between devices by JAX's collectives and lax.ppermute only.
A program may use at most 128 MiB of HBM per device.

```python
import math
import jax
import jax.numpy as jnp

HID = 14784
DW = 4096
R = 16
TOKEN_TOTAL = 12288


def shard_levels(stream_key, extent, split, smallest, high):
    def one(position, blocks):
        heights = jax.random.uniform(jax.random.fold_in(jax.random.fold_in(stream_key, 6), position), (blocks,), jnp.float32, smallest / len(split), high / len(split))
        return jnp.repeat(jnp.exp(heights), extent[position] // blocks).reshape((-1,) + (1,) * (len(extent) - position - 1))

    gain = one(*split[0])
    for cut in split[1:]:
        gain = gain * one(*cut)
    return gain


def gaussian(rng, dims, spread, reach, pieces=(), held_as=jnp.bfloat16):
    values = jax.random.normal(rng, dims, jnp.float32) * spread
    if len(pieces) > 0:
        values = shard_levels(rng, dims, pieces, -0.22, 0.18) * values
    return jnp.clip(values, min=-reach, max=reach).astype(held_as)


def setup_inputs(seed: int = 0) -> dict:
    streams_of = jax.random.split(jax.random.key(seed), 6)
    hidden = gaussian(streams_of[0], (TOKEN_TOTAL, HID), 1.0, 6.0, ((0, 32), (1, 8)))
    down_weight = gaussian(streams_of[1], (HID, DW), HID ** -0.5, 0.046875, ((0, 8), (1, 32)))
    adapter_in = gaussian(streams_of[2], (R, HID), HID ** -0.5, 0.046875, ((1, 8),))
    adapter_out = gaussian(streams_of[3], (R, DW), DW ** -0.5, 0.09375, ((1, 32),))
    cotangent = gaussian(streams_of[4], (TOKEN_TOTAL, DW), 1.0, 6.0, ((0, 32), (1, 8)))
    return {"hidden": hidden, "down_weight": down_weight, "adapter_in": adapter_in, "adapter_out": adapter_out, "cotangent": cotangent}


ADAPTER_SCALING = 2.0

def reference(hidden, down_weight, adapter_in, adapter_out, cotangent):
    rank_part = jnp.dot(hidden, adapter_in.T, preferred_element_type=jnp.float32)
    rank_round = rank_part.astype(jnp.bfloat16)
    main_contribution = jnp.dot(hidden, down_weight, preferred_element_type=jnp.float32)
    adapter_contribution = jnp.dot(rank_round, adapter_out, preferred_element_type=jnp.float32)
    projected = (main_contribution + ADAPTER_SCALING * adapter_contribution).astype(jnp.bfloat16)
    back_rank = jnp.dot(cotangent, adapter_out.T, preferred_element_type=jnp.float32).astype(jnp.bfloat16)
    backward_main_path = jnp.dot(cotangent, down_weight.T, preferred_element_type=jnp.float32)
    backward_adapter_path = jnp.dot(back_rank, adapter_in, preferred_element_type=jnp.float32)
    hidden_gradient = (backward_main_path + ADAPTER_SCALING * backward_adapter_path).astype(jnp.bfloat16)
    adapter_factor = ADAPTER_SCALING / math.sqrt(TOKEN_TOTAL)
    grad_in = adapter_factor * jnp.dot(back_rank.T, hidden, preferred_element_type=jnp.float32)
    grad_out = adapter_factor * jnp.dot(rank_round.T, cotangent, preferred_element_type=jnp.float32)
    return (projected, hidden_gradient, grad_in, grad_out)
```

```python
import math

import jax
import jax.numpy as jnp
from jax import lax
from jax.sharding import Mesh, PartitionSpec as P

SCALE = 2.0
PIPE = ("z", "x_hi", "core")
TENSOR = ("x_lo", "y")
NZ, NT = 8, 8
F32, BF16 = jnp.float32, jnp.bfloat16


def swap(x, axis):
    return lax.ppermute(x, axis, [(0, 1), (1, 0)])


def from_offset(x, k):
    return lax.ppermute(x, "z", [((i + k) % NZ, i) for i in range(NZ)])


def from_xor(x, axis, n, k):
    return lax.ppermute(x, axis, [(i ^ k, i) for i in range(n)])


def dot(a, b, ca, cb):
    return lax.dot_general(a, b, (((ca,), (cb,)), ((), ())), preferred_element_type=F32)


def flip_groups(parts, bit):
    a, b = parts
    return [jnp.where(bit == 0, a, b), jnp.where(bit == 0, b, a)]


def relative(x, x_hi, core):
    width = x.shape[1] // 4
    g = [x[:, i * width : (i + 1) * width] for i in range(4)]
    lo = flip_groups(g[:2], core)
    hi = flip_groups(g[2:], core)
    lo, hi = jnp.concatenate(lo, 1), jnp.concatenate(hi, 1)
    return jnp.concatenate(flip_groups([lo, hi], x_hi), 1)


def sum_over_tensor(x):
    for k in (1, 2, 4):
        x = x + from_xor(x, TENSOR, NT, k)
    return x


def sum_over_pipe(x):
    core, x_hi = lax.axis_index("core"), lax.axis_index("x_hi")
    width = x.shape[1] // 4

    def keep(x, bit, axis):
        half = x.shape[1] // 2
        mine = jnp.where(bit == 0, x[:, :half], x[:, half:])
        other = jnp.where(bit == 0, x[:, half:], x[:, :half])
        return mine + swap(other, axis)

    x = keep(x, core, "core")
    x = keep(x, x_hi, "x_hi")
    for k in (1, 2, 4):
        x = x + from_xor(x, "z", NZ, k)
    for bit, axis in ((x_hi, "x_hi"), (core, "core")):
        x = jnp.concatenate(flip_groups([x, swap(x, axis)], bit), 1)
    return x


def local(hidden, w, a_in, a_out, cot):
    z, x_hi, core = (lax.axis_index(a) for a in PIPE)
    t = lax.axis_index(TENSOR)
    tokens, units = hidden.shape

    g = jnp.concatenate([a_out, swap(a_out, "core")], 1)
    g = jnp.concatenate([g, swap(g, "x_hi")], 1)[None]
    for k in (1, 2, 4):
        g = jnp.concatenate([g, from_offset(g, k)], 0)
    factor = lax.dynamic_index_in_dim(g, (t - z) % NZ, 0, keepdims=False)

    cot_rel = relative(cot, x_hi, core)
    cots = lax.all_gather(cot_rel, TENSOR, axis=0)

    part = jnp.concatenate([dot(a_in, hidden, 1, 1), dot(factor, cot_rel, 1, 1)], 0)
    ranks = sum_over_tensor(part).astype(BF16)
    rank, back = ranks[:16], ranks[16:]
    c = SCALE / math.sqrt(tokens * 32)
    grads = jnp.concatenate([c * dot(back, hidden, 1, 0), c * dot(rank, cot, 1, 0)], 1)
    width = grads.shape[1]
    padded = -(-width // 512) * 512
    grads = sum_over_pipe(jnp.pad(grads, ((0, 0), (0, padded - width))))
    grad_in, grad_out = grads[:, :units], grads[:, units:width]

    cut = units // 2 // 16 * 16

    def chain(own, column, acc):
        shares = [None] * NZ

        def use(blocks, acc):
            for r, block in blocks:
                pair = jnp.concatenate([block, swap(block, "core")], 1)
                shares[r] = dot(hidden, pair, 1, 0).astype(BF16)
                left = lax.dynamic_index_in_dim(cots, (z + r) % NZ, 0, keepdims=False)
                left = left[:, column : column + pair.shape[1]]
                term = dot(left, pair, 1, 1)
                acc = term if acc is None else acc + term
            return acc

        acc = use([(0, own)], acc)
        up = down = own
        for s in range(1, NZ // 2):
            up, down = from_offset(up, 1), from_offset(down, -1)
            acc = use([(s, up), (NZ - s, down)], acc)
        last = jnp.concatenate([from_offset(up[:cut], 1), from_offset(down[cut:], -1)], 0)
        acc = use([(NZ // 2, last)], acc)
        return jnp.stack(shares), acc

    def scatter(shares):
        def pick(k):
            return lax.dynamic_index_in_dim(shares, ((t ^ k) - z) % NZ, 0, keepdims=False)

        total = pick(0).astype(F32)
        for k in range(1, NT):
            total = total + from_xor(pick(k), TENSOR, NT, k).astype(F32)
        return total

    shares_a, acc = chain(w, 0, None)
    main_a = scatter(shares_a)
    shares_b, acc = chain(swap(w, "x_hi"), 2 * w.shape[1], acc)
    main_b = scatter(shares_b)

    projected = jnp.concatenate([main_a, main_b], 1) + SCALE * dot(rank, factor, 0, 0)
    projected = relative(projected.astype(BF16), x_hi, core)
    hidden_gradient = (acc + SCALE * dot(back, a_in, 0, 0)).astype(BF16)
    return projected, hidden_gradient, grad_in, grad_out


def solution(mesh):
    fine = Mesh(mesh.devices.reshape(8, 2, 2, 2, 4), PIPE + TENSOR)
    return jax.shard_map(
        local,
        mesh=fine,
        in_specs=(P(PIPE, TENSOR), P(TENSOR, PIPE), P(None, TENSOR), P(None, PIPE), P(PIPE, TENSOR)),
        out_specs=(P(PIPE, TENSOR), P(PIPE, TENSOR), P(None, TENSOR), P(None, TENSOR)),
        check_vma=False,
    )
```

```python
import math

import jax
import jax.numpy as jnp
from jax import lax
from jax.experimental import pallas as pl
from jax.experimental.pallas import tpu as pltpu
from jax.sharding import Mesh, PartitionSpec as P

SCALE = 2.0
PIPE = ("z", "x_hi", "core")
TENSOR = ("x_lo", "y")
NZ, NT, NY = 8, 8, 4
F32, BF16 = jnp.float32, jnp.bfloat16


def swap(x, axis):
    return lax.ppermute(x, axis, [(0, 1), (1, 0)])


def from_offset(x, k):
    return lax.ppermute(x, "z", [((i + k) % NZ, i) for i in range(NZ)])


def from_xor(x, axis, n, k):
    return lax.ppermute(x, axis, [(i ^ k, i) for i in range(n)])


def dot(a, b, ca, cb):
    return lax.dot_general(a, b, (((ca,), (cb,)), ((), ())), preferred_element_type=F32)


together = lax.optimization_barrier


def flip(a, b, bit):
    return [jnp.where(bit == 0, a, b), jnp.where(bit == 0, b, a)]


def groups(x, x_hi, core):
    width = x.shape[1] // 4
    return [
        lax.dynamic_slice_in_dim(x, ((x_hi ^ i) * 2 + (core ^ j)) * width, width, 1)
        for i in range(2)
        for j in range(2)
    ]


def copy_kernel(at, in_ref, out_ref):
    out_ref[...] = in_ref[...]


def reorder(x, at):
    rows, group = x.shape[0], x.shape[1] // at.shape[0]
    return pl.pallas_call(
        copy_kernel,
        out_shape=jax.ShapeDtypeStruct(x.shape, x.dtype),
        grid_spec=pltpu.PrefetchScalarGridSpec(
            num_scalar_prefetch=1,
            grid=at.shape,
            in_specs=[pl.BlockSpec((rows, group), lambda i, at: (0, at[i]))],
            out_specs=pl.BlockSpec((rows, group), lambda i, at: (0, i)),
        ),
        compiler_params=pltpu.CompilerParams(vmem_limit_bytes=8 * 2**20),
        cost_estimate=pl.CostEstimate(flops=0, bytes_accessed=4 * x.size, transcendentals=0),
    )(at, x)


def local(hidden, w, a_in, a_out, cot):
    z, x_hi, core = (lax.axis_index(a) for a in PIPE)
    x_lo, y = (lax.axis_index(a) for a in TENSOR)
    t = x_lo * NY + y
    tokens, units = hidden.shape
    group = w.shape[1]

    all_w = lax.all_gather(w, "z", axis=1, tiled=True)

    def from_quad(x, k):
        return from_xor(x, ("x_hi", "core"), 4, k)

    cot_g = groups(cot, x_hi, core)
    mine = [cot_g[0]] + [from_quad(cot_g[k], k) for k in (2, 1, 3)]
    g = [a_out] + [from_quad(a_out, k) for k in range(1, 4)]
    mine = jnp.concatenate(mine, 0)
    g = jnp.concatenate(g, 1)[None]
    mine, g = together((mine, g))
    cot_t, hidden_own = together((jnp.concatenate([mine, swap(mine, "x_lo")], 1), hidden))
    hidden_x = swap(hidden_own, "x_hi")
    cots = [cot_t] + [from_xor(cot_t, "y", NY, k) for k in range(1, NY)]
    for k in (1, 2, 4):
        g = jnp.concatenate([g, from_offset(g, k)], 0)
    hidden_x, g, cots = together((hidden_x, g, cots))
    hidden_x = jnp.concatenate([hidden, hidden_x], 0)
    all_hidden = jnp.concatenate([hidden_x, swap(hidden_x, "core")], 0)
    cots = jnp.concatenate(cots, 1)

    cot_rel = jnp.concatenate(cot_g, 1)
    factor = lax.dynamic_index_in_dim(g, (t - z) % NZ, 0, keepdims=False)
    x = jnp.concatenate([dot(a_in, hidden, 1, 1), dot(factor, cot_rel, 1, 1)], 0)
    for k in (1, 2, 4):
        x = x + from_xor(x, TENSOR, NT, k)
    ranks = x.astype(BF16)

    cots, all_w, ranks, all_hidden = together((cots, all_w, ranks, all_hidden))
    at = [(x_lo ^ i) * NY + (y ^ k) for k in range(NY) for i in range(2)]
    all_w = reorder(all_w, jnp.stack(at))

    def forward(k):
        return dot(all_hidden, all_w[:, 2 * k * group : 2 * (k + 1) * group], 1, 0).astype(BF16)

    def backward(first, last):
        return dot(cots[first * tokens : last * tokens], all_w, 1, 1)

    got, all_hidden = together((backward(2, 4).astype(BF16), all_hidden))
    got = swap(got, "core")
    shares = {1: forward(1), 3: forward(3)}
    rank, back = ranks[:16], ranks[16:]
    c = SCALE / math.sqrt(tokens * 32)
    grads = jnp.concatenate([c * dot(back, hidden, 1, 0), c * dot(rank, cot, 1, 0)], 1)
    grads = grads + swap(grads, "core")
    rank_x = jnp.concatenate([rank, swap(rank, "x_hi")], 1)
    all_rank = jnp.concatenate([rank_x, swap(rank_x, "core")], 1)
    got, shares, cots, all_hidden, all_rank = together((got, shares, cots, all_hidden, all_rank))
    sent = {k: from_xor(shares[k], "y", NY, k) for k in (1, 3)}
    give = (backward(1, 2) + got[tokens:].astype(F32)).astype(BF16)
    give, all_hidden = together((give, all_hidden))
    last = swap(give, "x_hi")
    shares = {2: forward(2), 0: forward(0)}
    sent[2] = from_xor(shares[2], "y", NY, 2)
    cots, main, last, grads = together((cots, shares[0], last, grads))
    own = backward(0, 1) + got[:tokens].astype(F32) + SCALE * dot(back, a_in, 0, 0)
    for k in (1, 2, 4):
        grads = grads + from_xor(grads, "z", NZ, k)
    grads = grads + swap(grads, "x_hi")
    main, own = together((main, own))

    main = main.astype(F32)
    for k in (1, 3, 2):
        main = main + sent[k].astype(F32)
    main = main[:, :group] + swap(main[:, group:].astype(BF16), "x_lo").astype(F32)
    out = (main + SCALE * dot(all_rank, factor[:, :group], 0, 0)).astype(BF16)
    out = jnp.concatenate([out[: 2 * tokens], swap(out[2 * tokens :], "core")], 1)
    out = jnp.concatenate([out[:tokens], swap(out[tokens:], "x_hi")], 1)
    projected = jnp.concatenate(groups(out, x_hi, core), 1)
    hidden_gradient = (own + last.astype(F32)).astype(BF16)
    return projected, hidden_gradient, grads[:, :units], grads[:, units:]


def solution(mesh):
    fine = Mesh(mesh.devices.reshape(8, 2, 2, 2, 4), PIPE + TENSOR)
    return jax.shard_map(
        local,
        mesh=fine,
        in_specs=(P(PIPE, TENSOR), P(TENSOR, PIPE), P(None, TENSOR), P(None, PIPE), P(PIPE, TENSOR)),
        out_specs=(P(PIPE, TENSOR), P(PIPE, TENSOR), P(None, TENSOR), P(None, TENSOR)),
        check_vma=False,
    )
```

```python
import math

import jax
import jax.numpy as jnp
from jax import lax
from jax.experimental import pallas as pl
from jax.experimental.pallas import tpu as pltpu
from jax.sharding import Mesh, PartitionSpec as P

SCALE = 2.0
PIPE = ("z", "x_hi", "core")
TENSOR = ("x_lo", "y")
NZ, NT, NY = 8, 8, 4
F32, BF16 = jnp.float32, jnp.bfloat16


def swap(x, axis):
    return lax.ppermute(x, axis, [(0, 1), (1, 0)])


def from_offset(x, k):
    return lax.ppermute(x, "z", [((i + k) % NZ, i) for i in range(NZ)])


def from_xor(x, axis, n, k):
    return lax.ppermute(x, axis, [(i ^ k, i) for i in range(n)])


def dot(a, b, ca, cb):
    return lax.dot_general(a, b, (((ca,), (cb,)), ((), ())), preferred_element_type=F32)


together = lax.optimization_barrier


def flip(a, b, bit):
    return [jnp.where(bit == 0, a, b), jnp.where(bit == 0, b, a)]


def groups(x, x_hi, core):
    width = x.shape[1] // 4
    return [
        lax.dynamic_slice_in_dim(x, ((x_hi ^ i) * 2 + (core ^ j)) * width, width, 1)
        for i in range(2)
        for j in range(2)
    ]


def copy_kernel(at, in_ref, out_ref):
    out_ref[...] = in_ref[...]


def reorder(x, at):
    rows, group = x.shape[0], x.shape[1] // at.shape[0]
    return pl.pallas_call(
        copy_kernel,
        out_shape=jax.ShapeDtypeStruct(x.shape, x.dtype),
        grid_spec=pltpu.PrefetchScalarGridSpec(
            num_scalar_prefetch=1,
            grid=at.shape,
            in_specs=[pl.BlockSpec((rows, group), lambda i, at: (0, at[i]))],
            out_specs=pl.BlockSpec((rows, group), lambda i, at: (0, i)),
        ),
        compiler_params=pltpu.CompilerParams(vmem_limit_bytes=8 * 2**20),
        cost_estimate=pl.CostEstimate(flops=0, bytes_accessed=4 * x.size, transcendentals=0),
    )(at, x)


def local(hidden, w, a_in, a_out, cot):
    z, x_hi, core = (lax.axis_index(a) for a in PIPE)
    x_lo, y = (lax.axis_index(a) for a in TENSOR)
    t = x_lo * NY + y
    tokens, units = hidden.shape
    group = w.shape[1]

    all_w = lax.all_gather(w, "z", axis=1, tiled=True)

    def from_quad(x, k):
        return from_xor(x, ("x_hi", "core"), 4, k)

    cot_g = groups(cot, x_hi, core)
    mine = [cot_g[0]] + [from_quad(cot_g[k], k) for k in (2, 1, 3)]
    g = [a_out] + [from_quad(a_out, k) for k in range(1, 4)]
    mine = jnp.concatenate(mine, 0)
    g = jnp.concatenate(g, 1)[None]
    mine, g = together((mine, g))
    swapped = swap(mine, "x_lo")
    near = [from_xor(mine, "y", NY, k) for k in (1, 3)]
    swapped, near, mine, hidden_own = together((swapped, near, mine, hidden))
    hidden_x = swap(hidden_own, "x_hi")
    far = from_xor(jnp.concatenate([mine, swapped], 1), "y", NY, 2)
    others = [from_xor(swapped, "y", NY, k) for k in (1, 3)]
    cots = [mine, swapped, near[0], others[0], far, near[1], others[1]]
    for k in (1, 2, 4):
        g = jnp.concatenate([g, from_offset(g, k)], 0)
    hidden_x, g, cots = together((hidden_x, g, cots))

    hidden_x = jnp.concatenate([hidden, hidden_x], 0)
    hidden_c = swap(hidden_x, "core")
    cot_rel = jnp.concatenate(cot_g, 1)
    factor = lax.dynamic_index_in_dim(g, (t - z) % NZ, 0, keepdims=False)
    x = jnp.concatenate([dot(a_in, hidden, 1, 1), dot(factor, cot_rel, 1, 1)], 0)
    x = x + from_xor(x, TENSOR, NT, 1)
    x, cots = together((x, jnp.concatenate(cots, 1)))
    x = x + from_xor(x, TENSOR, NT, 2)
    at = [(x_lo ^ i) * NY + (y ^ k) for k in range(NY) for i in range(2)]
    x, all_w = together((x, reorder(all_w, jnp.stack(at))))
    x = x + from_xor(x, TENSOR, NT, 4)
    x, all_hidden = together((x, jnp.concatenate([hidden_x, hidden_c], 0)))
    ranks = x.astype(BF16)

    cots, all_w, all_hidden = together((cots, all_w, all_hidden))

    def forward(k):
        return dot(all_hidden, all_w[:, 2 * k * group : 2 * (k + 1) * group], 1, 0).astype(BF16)

    def backward(first, last):
        return dot(cots[first * tokens : last * tokens], all_w, 1, 1)

    got, all_hidden = together((backward(2, 4).astype(BF16), all_hidden))
    got = swap(got, "core")
    shares = {1: forward(1), 3: forward(3)}
    rank, back = ranks[:16], ranks[16:]
    c = SCALE / math.sqrt(tokens * 32)
    grads = jnp.concatenate([c * dot(back, hidden, 1, 0), c * dot(rank, cot, 1, 0)], 1)
    grads = grads + swap(grads, "core")
    all_grads = lax.all_gather(grads, "z", axis=0)
    rank_x = jnp.concatenate([rank, swap(rank, "x_hi")], 1)
    all_rank = jnp.concatenate([rank_x, swap(rank_x, "core")], 1)
    got, shares, cots, all_hidden, all_rank = together((got, shares, cots, all_hidden, all_rank))
    sent = {k: from_xor(shares[k], "y", NY, k) for k in (1, 3)}
    give = (backward(1, 2) + got[tokens:].astype(F32)).astype(BF16)
    give, all_hidden = together((give, all_hidden))
    last = swap(give, "x_hi")
    shares = together({2: forward(2), 0: forward(0)})
    sent[2] = from_xor(shares[2], "y", NY, 2)
    main, last, sent[1], sent[3], cots = together((shares[0], last, sent[1], sent[3], cots))
    grads = jnp.sum(all_grads, 0)
    grads = grads + swap(grads, "x_hi")

    main = main.astype(F32)
    for k in (1, 3, 2):
        main = main + sent[k].astype(F32)
    main = main[:, :group] + swap(main[:, group:].astype(BF16), "x_lo").astype(F32)
    out = (main + SCALE * dot(all_rank, factor[:, :group], 0, 0)).astype(BF16)
    rows = {0: 0, 2: 1, 1: 2, 3: 3}
    out = {k: out[i * tokens : (i + 1) * tokens] for k, i in rows.items()}
    out = [out[0]] + [from_quad(out[k], k) for k in range(1, 4)]
    projected = jnp.concatenate(groups(jnp.concatenate(out, 1), x_hi, core), 1)
    own = backward(0, 1) + got[:tokens].astype(F32) + SCALE * dot(back, a_in, 0, 0)
    hidden_gradient = (own + last.astype(F32)).astype(BF16)
    return projected, hidden_gradient, grads[:, :units], grads[:, units:]


def solution(mesh):
    fine = Mesh(mesh.devices.reshape(8, 2, 2, 2, 4), PIPE + TENSOR)
    return jax.shard_map(
        local,
        mesh=fine,
        in_specs=(P(PIPE, TENSOR), P(TENSOR, PIPE), P(None, TENSOR), P(None, PIPE), P(PIPE, TENSOR)),
        out_specs=(P(PIPE, TENSOR), P(PIPE, TENSOR), P(None, TENSOR), P(None, TENSOR)),
        check_vma=False,
    )
```

```python
import math

import jax
import jax.numpy as jnp
from jax import lax
from jax.experimental import pallas as pl
from jax.experimental.pallas import tpu as pltpu
from jax.sharding import Mesh, PartitionSpec as P

SCALE = 2.0
PIPE = ("z", "x_hi", "core")
TENSOR = ("x_lo", "y")
NZ, NT, NY = 8, 8, 4
F32, BF16 = jnp.float32, jnp.bfloat16


def swap(x, axis):
    return lax.ppermute(x, axis, [(0, 1), (1, 0)])


def from_offset(x, k):
    return lax.ppermute(x, "z", [((i + k) % NZ, i) for i in range(NZ)])


def from_xor(x, axis, n, k):
    return lax.ppermute(x, axis, [(i ^ k, i) for i in range(n)])


def dot(a, b, ca, cb):
    return lax.dot_general(a, b, (((ca,), (cb,)), ((), ())), preferred_element_type=F32)


together = lax.optimization_barrier


def flip(a, b, bit):
    return [jnp.where(bit == 0, a, b), jnp.where(bit == 0, b, a)]


def groups(x, x_hi, core):
    width = x.shape[1] // 4
    return [
        lax.dynamic_slice_in_dim(x, ((x_hi ^ i) * 2 + (core ^ j)) * width, width, 1)
        for i in range(2)
        for j in range(2)
    ]


def copy_kernel(at, in_ref, out_ref):
    out_ref[...] = in_ref[...]


def reorder(x, at):
    rows, group = x.shape[0], x.shape[1] // at.shape[0]
    return pl.pallas_call(
        copy_kernel,
        out_shape=jax.ShapeDtypeStruct(x.shape, x.dtype),
        grid_spec=pltpu.PrefetchScalarGridSpec(
            num_scalar_prefetch=1,
            grid=at.shape,
            in_specs=[pl.BlockSpec((rows, group), lambda i, at: (0, at[i]))],
            out_specs=pl.BlockSpec((rows, group), lambda i, at: (0, i)),
        ),
        compiler_params=pltpu.CompilerParams(vmem_limit_bytes=8 * 2**20),
        cost_estimate=pl.CostEstimate(flops=0, bytes_accessed=4 * x.size, transcendentals=0),
    )(at, x)


def local(hidden, w, a_in, a_out, cot):
    z, x_hi, core = (lax.axis_index(a) for a in PIPE)
    x_lo, y = (lax.axis_index(a) for a in TENSOR)
    t = x_lo * NY + y
    tokens, units = hidden.shape
    group = w.shape[1]

    all_w = lax.all_gather(w, "z", axis=1, tiled=True)

    def from_quad(x, k):
        return from_xor(x, ("x_hi", "core"), 4, k)

    cot_g = groups(cot, x_hi, core)
    mine = [cot_g[0]] + [from_quad(cot_g[k], k) for k in (2, 1, 3)]
    g = [a_out] + [from_quad(a_out, k) for k in range(1, 4)]
    mine = jnp.concatenate(mine, 0)
    g = jnp.concatenate(g, 1)[None]
    mine, g = together((mine, g))
    swapped = swap(mine, "x_lo")
    near = [from_xor(mine, "y", NY, k) for k in (1, 3)]
    swapped, near, mine, hidden_own = together((swapped, near, mine, hidden))
    hidden_x = swap(hidden_own, "x_hi")
    far = from_xor(jnp.concatenate([mine, swapped], 1), "y", NY, 2)
    others = [from_xor(swapped, "y", NY, k) for k in (1, 3)]
    cots = [mine, swapped, near[0], others[0], far, near[1], others[1]]
    for k in (1, 2, 4):
        g = jnp.concatenate([g, from_offset(g, k)], 0)
    hidden_x, g, cots = together((hidden_x, g, cots))

    hidden_x = jnp.concatenate([hidden, hidden_x], 0)
    hidden_c = swap(hidden_x, "core")
    cot_rel = jnp.concatenate(cot_g, 1)
    factor = lax.dynamic_index_in_dim(g, (t - z) % NZ, 0, keepdims=False)
    x = jnp.concatenate([dot(a_in, hidden, 1, 1), dot(factor, cot_rel, 1, 1)], 0)
    x = x + from_xor(x, TENSOR, NT, 1)
    x, cots = together((x, jnp.concatenate(cots, 1)))
    x = x + from_xor(x, TENSOR, NT, 2)
    at = [(x_lo ^ i) * NY + (y ^ k) for k in range(NY) for i in range(2)]
    x, all_w = together((x, reorder(all_w, jnp.stack(at))))
    x = x + from_xor(x, TENSOR, NT, 4)
    x, all_hidden = together((x, jnp.concatenate([hidden_x, hidden_c], 0)))
    ranks = x.astype(BF16)

    cots, all_w, all_hidden = together((cots, all_w, all_hidden))

    def forward(k):
        return dot(all_hidden, all_w[:, 2 * k * group : 2 * (k + 1) * group], 1, 0).astype(BF16)

    def backward(first, last):
        return dot(cots[first * tokens : last * tokens], all_w, 1, 1)

    got, all_hidden = together((backward(2, 4).astype(BF16), all_hidden))
    got = swap(got, "core")
    shares = {1: forward(1), 3: forward(3)}
    rank, back = ranks[:16], ranks[16:]
    c = SCALE / math.sqrt(tokens * 32)
    grads = jnp.concatenate([c * dot(back, hidden, 1, 0), c * dot(rank, cot, 1, 0)], 1)
    got, shares, cots, all_hidden = together((got, shares, cots, all_hidden))
    sent = {k: from_xor(shares[k], "y", NY, k) for k in (1, 3)}
    give = (backward(1, 2) + got[tokens:].astype(F32)).astype(BF16)
    give, all_hidden, grads = together((give, all_hidden, grads))
    grads = grads + swap(grads, "core")
    all_grads = lax.all_gather(grads, "z", axis=0)
    last = swap(give, "x_hi")
    shares = together({2: forward(2), 0: forward(0)})
    sent[2] = from_xor(shares[2], "y", NY, 2)
    last, sent[1], rank = together((last, sent[1], rank))
    all_rank = [from_quad(rank, k) for k in range(1, 4)]
    all_rank = jnp.concatenate([rank, all_rank[1], all_rank[0], all_rank[2]], 1)
    main, sent[3], cots, all_rank = together((shares[0], sent[3], cots, all_rank))

    main = main.astype(F32)
    for k in (1, 3, 2):
        main = main + sent[k].astype(F32)
    main, all_grads = together((main, all_grads))
    grads = jnp.sum(all_grads, 0)
    grads = grads + swap(grads, "x_hi")
    main = main[:, :group] + swap(main[:, group:].astype(BF16), "x_lo").astype(F32)
    out = (main + SCALE * dot(all_rank, factor[:, :group], 0, 0)).astype(BF16)
    rows = {0: 0, 2: 1, 1: 2, 3: 3}
    out = {k: out[i * tokens : (i + 1) * tokens] for k, i in rows.items()}
    out = [out[0]] + [from_quad(out[k], k) for k in range(1, 4)]
    projected = jnp.concatenate(groups(jnp.concatenate(out, 1), x_hi, core), 1)
    own = backward(0, 1) + got[:tokens].astype(F32) + SCALE * dot(back, a_in, 0, 0)
    hidden_gradient = (own + last.astype(F32)).astype(BF16)
    return projected, hidden_gradient, grads[:, :units], grads[:, units:]


def solution(mesh):
    fine = Mesh(mesh.devices.reshape(8, 2, 2, 2, 4), PIPE + TENSOR)
    return jax.shard_map(
        local,
        mesh=fine,
        in_specs=(P(PIPE, TENSOR), P(TENSOR, PIPE), P(None, TENSOR), P(None, PIPE), P(PIPE, TENSOR)),
        out_specs=(P(PIPE, TENSOR), P(PIPE, TENSOR), P(None, TENSOR), P(None, TENSOR)),
        check_vma=False,
    )
```
